32 devices in a mesh: ply: 4 (over y, x), tile: 8 (over z, core).
Axes of the slice: x: 2, y: 2, z: 4, core: 2. Of those that a mesh axis runs over, the one named last changes fastest.
Arguments:
- scaled_warmth: float32 [16, 64, 1024], P('ply', 'tile'), may hold values from 0.9 to 1.1
- crosslink_fraction: float32 [16, 64, 1024], P('ply', 'tile'), may hold values from 0 to 0.4
- fluid_stress: float32 [16, 64, 1024], P('ply', 'tile'), may hold values from 0 to 1
- preform_porosity_coefficient: float32 [16, 64, 1024], P('ply', 'tile'), may hold values from 0.02 to 0.2
- wetted_flags: int32 [16, 64, 1024], P('ply', 'tile'), may hold values 0 or 1
- injection_flags: int32 [16, 64, 1024], P('ply', 'tile'), may hold values 0 or 1
- outlet_flags: int32 [16, 64, 1024], P('ply', 'tile'), may hold values 0 or 1
Outputs:
- temperature_out: float32 [16, 64, 1024], P('ply', 'tile')
- cure_out: float32 [16, 64, 1024], P('ply', 'tile')
- pressure_out: float32 [16, 64, 1024], P('ply', 'tile')
- imbalance_record: float32 [2], replicated
The draws below stay inside these ranges and needn't reach their ends.
All inputs are finite; a program needn't handle non-finite values. No bound on the sum of `wetted_flags` or of `injection_flags` or of `outlet_flags` on one device may be relied on, other than what follows from the above.
Results may differ from the reference program's by a relative error of at most 0.0003.
Values sent between devices are 32-bit elements; how exact they have to be, the bound alone decides.
A program may use at most 64 MiB of HBM per device.

```python
import math
import jax
import jax.numpy as jnp

GRID_CROSSWISE = 1024
STEPS = 2
SWEEPS = 4
LAMINA_TOTAL = 16
GRID_LENGTHWISE = 64


def plant(entries, rng, smallest, high):
    dims = entries.shape
    spot = [jax.random.randint(jax.random.fold_in(rng, axis), (), 0, dims[axis]) for axis in range(len(dims))]
    entries = entries.at[tuple(spot)].set(smallest)
    longest = dims.index(max(dims))
    spot[longest] = (spot[longest] + 1) % dims[longest]
    return entries.at[tuple(spot)].set(high)


def levels(key, dims, pieces, least, top_value):
    gain = 1.0
    for dim, shards_of in pieces:
        steps = jax.random.uniform(jax.random.fold_in(jax.random.fold_in(key, 6), dim), (shards_of,), jnp.float32, least / len(pieces), top_value / len(pieces))
        gain = gain * jnp.repeat(jnp.exp(steps), dims[dim] // shards_of).reshape((-1,) + (1,) * (len(dims) - 1 - dim))
    return gain


def setup_inputs(seed: int = 0) -> dict:
    arg_keys = jax.random.split(jax.random.key(seed), 8)
    scaled_warmth = jnp.clip(0.9 + 0.20000005 * jax.random.uniform(arg_keys[0], (LAMINA_TOTAL, GRID_LENGTHWISE, GRID_CROSSWISE), jnp.float32) ** levels(arg_keys[0], (LAMINA_TOTAL, GRID_LENGTHWISE, GRID_CROSSWISE), ((0, 4), (1, 8)), -0.2, 0.2), 0.9, 1.1)
    crosslink_fraction = jnp.clip(0.4 * jax.random.uniform(arg_keys[1], (LAMINA_TOTAL, GRID_LENGTHWISE, GRID_CROSSWISE), jnp.float32) ** levels(arg_keys[1], (LAMINA_TOTAL, GRID_LENGTHWISE, GRID_CROSSWISE), ((0, 4), (1, 8)), -0.2, 0.2), 0.0, 0.4)
    fluid_stress = jnp.clip(1.0 * jax.random.uniform(arg_keys[2], (LAMINA_TOTAL, GRID_LENGTHWISE, GRID_CROSSWISE), jnp.float32) ** levels(arg_keys[2], (LAMINA_TOTAL, GRID_LENGTHWISE, GRID_CROSSWISE), ((0, 4), (1, 8)), -0.2, 0.2), 0.0, 1.0)
    preform_porosity_coefficient = jnp.clip(jnp.exp(math.log(0.2) - 2.3025851 * jax.random.uniform(arg_keys[3], (LAMINA_TOTAL, GRID_LENGTHWISE, GRID_CROSSWISE), jnp.float32) ** levels(arg_keys[3], (LAMINA_TOTAL, GRID_LENGTHWISE, GRID_CROSSWISE), ((0, 4), (1, 8)), -0.2, 0.2)), 0.02, 0.2)
    wetted_flags = plant((jax.random.randint(arg_keys[4], (LAMINA_TOTAL, GRID_LENGTHWISE, GRID_CROSSWISE), 0, 4) < 3).astype(jnp.int32), jax.random.fold_in(arg_keys[4], 1), 0, 1)
    injection_flags = plant((jax.random.randint(arg_keys[5], (LAMINA_TOTAL, GRID_LENGTHWISE, GRID_CROSSWISE), 0, 32) < 1).astype(jnp.int32), jax.random.fold_in(arg_keys[5], 1), 0, 1)
    outlet_flags = plant((jax.random.randint(arg_keys[6], (LAMINA_TOTAL, GRID_LENGTHWISE, GRID_CROSSWISE), 0, 32) < 1).astype(jnp.int32), jax.random.fold_in(arg_keys[6], 1), 0, 1)
    return dict(scaled_warmth=scaled_warmth, crosslink_fraction=crosslink_fraction, fluid_stress=fluid_stress, preform_porosity_coefficient=preform_porosity_coefficient, wetted_flags=wetted_flags, injection_flags=injection_flags, outlet_flags=outlet_flags)


fluidity_barrier = 4.0
fluidity_gelation_coefficient = 2.0
arrhenius_prefactor = 0.2
arrhenius_barrier = 8.0
released_enthalpy = 0.3
diffusion_coefficient = 0.1
clock_step_size = 0.5
epsilon = 1e-06

def interior(array):
    return array[1:-1, 1:-1, 1:-1]

def nearby_sites(array):
    return [array[2:, 1:-1, 1:-1], array[:-2, 1:-1, 1:-1], array[1:-1, 2:, 1:-1], array[1:-1, :-2, 1:-1], array[1:-1, 1:-1, 2:], array[1:-1, 1:-1, :-2]]

def face_mobility(mobility_pad):
    centre = interior(mobility_pad)
    result = []
    for beside in nearby_sites(mobility_pad):
        denom = centre + beside
        result.append(2.0 * centre * beside / jnp.where(denom > 0, denom, 1.0))
    return result

def jacobi_sweep(pressure_pad, boundary_sides, dry_site, fixed_value):
    beside = nearby_sites(pressure_pad)
    weighted = boundary_sides[0] * beside[0]
    diagonal_sum = boundary_sides[0]
    for iteration_counter in range(1, 6):
        weighted = weighted + boundary_sides[iteration_counter] * beside[iteration_counter]
        diagonal_sum = diagonal_sum + boundary_sides[iteration_counter]
    return jnp.where(dry_site > 0, weighted / jnp.where(dry_site > 0, diagonal_sum, 1.0), fixed_value)

def donor_advection(fluid_stress, scaled_warmth, crosslink_fraction, boundary_sides, nearby_stress, nearby_warmth, nearby_crosslink, wetted_status, nearby_wetted, dry_site):
    weighted = boundary_sides[0] * nearby_stress[0]
    diagonal_sum = boundary_sides[0]
    for iteration_counter in range(1, 6):
        weighted = weighted + boundary_sides[iteration_counter] * nearby_stress[iteration_counter]
        diagonal_sum = diagonal_sum + boundary_sides[iteration_counter]
    darcy_imbalance = dry_site * (weighted - diagonal_sum * fluid_stress)
    donor_warmth_advance = jnp.zeros_like(scaled_warmth)
    donor_crosslink_advance = jnp.zeros_like(scaled_warmth)
    diffusive_stream = jnp.zeros_like(scaled_warmth)
    for iteration_counter in range(6):
        inward_stream = jnp.maximum(boundary_sides[iteration_counter] * (nearby_stress[iteration_counter] - fluid_stress), 0.0) * nearby_wetted[iteration_counter]
        donor_warmth_advance = donor_warmth_advance + inward_stream * (nearby_warmth[iteration_counter] - scaled_warmth)
        donor_crosslink_advance = donor_crosslink_advance + inward_stream * (nearby_crosslink[iteration_counter] - crosslink_fraction)
        diffusive_stream = diffusive_stream + nearby_wetted[iteration_counter] * (nearby_warmth[iteration_counter] - scaled_warmth)
    crosslink_speed = arrhenius_prefactor * jnp.exp(arrhenius_barrier * (1.0 - 1.0 / scaled_warmth)) * (1.0 - crosslink_fraction)
    advanced_warmth = scaled_warmth + wetted_status * clock_step_size * (donor_warmth_advance + diffusion_coefficient * diffusive_stream + released_enthalpy * crosslink_speed)
    advanced_crosslink = crosslink_fraction + wetted_status * clock_step_size * (donor_crosslink_advance + crosslink_speed)
    return (darcy_imbalance, advanced_warmth, advanced_crosslink)

def reference(scaled_warmth, crosslink_fraction, fluid_stress, preform_porosity_coefficient, wetted_flags, injection_flags, outlet_flags):
    wetted_status = wetted_flags.astype(jnp.float32)
    inlet_cell = injection_flags.astype(jnp.float32)
    dry_site = wetted_status * (1.0 - inlet_cell) * (1.0 - outlet_flags.astype(jnp.float32))
    nearby_wetted = nearby_sites(jnp.pad(wetted_status, 1))
    gathered_magnitudes = []
    for repeat in range(STEPS):
        fluid_conductance = preform_porosity_coefficient * jnp.exp(-(fluidity_barrier * (1.0 / scaled_warmth - 1.0) + fluidity_gelation_coefficient * crosslink_fraction))
        boundary_sides = face_mobility(jnp.pad(fluid_conductance, 1))
        for sweep_index in range(SWEEPS):
            fluid_stress = jacobi_sweep(jnp.pad(fluid_stress, 1), boundary_sides, dry_site, inlet_cell)
        darcy_imbalance, scaled_warmth, crosslink_fraction = donor_advection(fluid_stress, scaled_warmth, crosslink_fraction, boundary_sides, nearby_sites(jnp.pad(fluid_stress, 1)), nearby_sites(jnp.pad(scaled_warmth, 1)), nearby_sites(jnp.pad(crosslink_fraction, 1)), wetted_status, nearby_wetted, dry_site)
        gathered_magnitudes.append(jnp.sqrt(jnp.sum(darcy_imbalance * darcy_imbalance) / darcy_imbalance.size + epsilon))
    return (scaled_warmth, crosslink_fraction, fluid_stress, jnp.stack(gathered_magnitudes))
```

```python
import functools

import jax
import jax.numpy as jnp
from jax import lax
from jax.experimental import pallas as pl
from jax.experimental.pallas import tpu as pltpu
from jax.sharding import PartitionSpec as P

STEPS = 2
SWEEPS = 4

fluidity_barrier = 4.0
fluidity_gelation_coefficient = 2.0
arrhenius_prefactor = 0.2
arrhenius_barrier = 8.0
released_enthalpy = 0.3
diffusion_coefficient = 0.1
clock_step_size = 0.5
epsilon = 1e-06

MESH = pl.DeviceIdType.MESH
PER_STEP = SWEEPS + 3
MESSAGES = 2 + STEPS * PER_STEP


def mobility_of(warmth, cure, preform):
    return preform * jnp.exp(
        -(fluidity_barrier * (1.0 / warmth - 1.0) + fluidity_gelation_coefficient * cure)
    )


def face(m, k):
    denom = m + k
    return 2.0 * m * k / jnp.where(denom > 0, denom, 1.0)


def kernel(
    n_ply, n_tile,
    t_in, c_in, p_in, k_in, w_in, i_in, o_in,
    t_out, c_out, p_out, rec_out,
    tb, cb, pb, mb, kb, flags, fill, free, fixed, fills, fz, fy, fx, fh, diag, inv, acc, part,
    hp, hr, red, half, tot,
    in_sem, out_sem, send_sem, recv_sem, rs_sem, rr_sem, qs_sem, qr_sem,
):
    planes, rows, width = p_in.shape
    ply, tile = lax.axis_index("ply"), lax.axis_index("tile")
    sites = planes * rows * width * n_ply * n_tile

    ins = [
        pltpu.make_async_copy(src, dst, in_sem.at[n])
        for n, (src, dst) in enumerate(
            [(p_in, pb.at[0]), (t_in, tb.at[0]), (c_in, cb.at[0]), (k_in, kb),
             (w_in, flags.at[0]), (i_in, flags.at[1]), (o_in, flags.at[2])]
        )
    ]
    for copy in ins:
        copy.start()

    barrier = pltpu.get_barrier_semaphore()
    for off in range(1, n_ply):
        pl.semaphore_signal(
            barrier, inc=1, device_id=(lax.rem(ply + off, n_ply), tile), device_id_type=MESH
        )

    def greet(off, carry):
        pl.semaphore_signal(
            barrier, inc=1, device_id=(ply, lax.rem(tile + off, n_tile)), device_id_type=MESH
        )
        return carry

    lax.fori_loop(1, n_tile, greet, 0)
    pl.semaphore_wait(barrier, n_ply + n_tile - 2)

    has = [ply < n_ply - 1, ply > 0, tile < n_tile - 1, tile > 0]

    def message(m, src, d):
        if d < 2:
            edge = 0 if d == 0 else planes - 1
            a, b = src.at[edge], hp.at[m, 1 - d]
            where = (ply - 1 if d == 0 else ply + 1, tile)
        else:
            lo, hi = pl.ds(0, 1), pl.ds(rows - 1, 1)
            a = src.at[:, lo if d == 2 else hi]
            b = hr.at[m, :, hi if d == 2 else lo]
            where = (ply, tile - 1 if d == 2 else tile + 1)
        return pltpu.make_async_remote_copy(
            src_ref=a, dst_ref=b, send_sem=send_sem.at[m, d], recv_sem=recv_sem.at[m, d],
            device_id=where, device_id_type=MESH,
        )

    opposite = [1, 0, 3, 2]

    def send(m, src, ds=(0, 1, 2, 3)):
        for d in ds:
            pl.when(has[opposite[d]])(lambda d=d: message(m, src, d).start())

    def landed(m, src, ds):
        for d in ds:
            pl.when(has[d])(lambda d=d: message(m, src, d).wait_recv())

    def sent(m, src):
        for d in range(4):
            pl.when(has[opposite[d]])(lambda d=d: message(m, src, d).wait_send())

    row = lax.broadcasted_iota(jnp.int32, (rows, width), 0)
    lane = lax.broadcasted_iota(jnp.int32, (rows, width), 1)
    first_row, last_row = row == 0, row == rows - 1
    edge_row = (first_row & (tile > 0)) | (last_row & (tile < n_tile - 1))
    first_lane, last_lane = lane == 0, lane == width - 1

    def up(x, axis):
        return pltpu.roll(x, x.shape[axis] - 1, axis)

    def down(x, axis):
        return pltpu.roll(x, 1, axis)

    def low_plane(m):
        return jnp.where(ply > 0, hp[m, 0], 0.0)

    def high_plane(m):
        return jnp.where(ply < n_ply - 1, hp[m, 1], 0.0)

    def edge_rows(m, p):
        return jnp.where(edge_row, hr[m, p], 0.0)

    P0, FILL = 0, 1
    MOB = [2 + s * PER_STEP for s in range(STEPS)]
    WARM = [m + 1 for m in MOB]
    CURE = [m + 2 for m in MOB]
    PRESS = [[MOB[s] + 3 + k for k in range(SWEEPS)] for s in range(STEPS)]
    sources = {P0: pb.at[0], FILL: fill}
    for s in range(STEPS):
        sources[MOB[s]], sources[WARM[s]], sources[CURE[s]] = mb.at[s], tb.at[s], cb.at[s]
        for k in range(SWEEPS):
            sources[PRESS[s][k]] = pb.at[s * SWEEPS + k + 1]

    def reduce_send(s):
        def body(off, carry):
            pltpu.make_async_remote_copy(
                src_ref=part.at[s], dst_ref=red.at[s, tile],
                send_sem=rs_sem.at[s, off], recv_sem=rr_sem.at[s, tile],
                device_id=(ply, lax.rem(tile + off, n_tile)), device_id_type=MESH,
            ).start()
            return carry

        lax.fori_loop(1, n_tile, body, 0)

    def reduce_mid(s):
        def body(off, total):
            peer = lax.rem(tile + off, n_tile)
            copy = pltpu.make_async_remote_copy(
                src_ref=part.at[s], dst_ref=red.at[s, peer],
                send_sem=rs_sem.at[s, off], recv_sem=rr_sem.at[s, peer],
                device_id=(ply, peer), device_id_type=MESH,
            )
            copy.wait_recv()
            copy.wait_send()
            return total + red[s, peer]

        half[s] = lax.fori_loop(1, n_tile, body, part[s])
        for off in range(1, n_ply):
            pltpu.make_async_remote_copy(
                src_ref=half.at[s], dst_ref=tot.at[s, ply],
                send_sem=qs_sem.at[s, off], recv_sem=qr_sem.at[s, ply],
                device_id=(lax.rem(ply + off, n_ply), tile), device_id_type=MESH,
            ).start()

    def reduce_end(s):
        tot[s, ply] = half[s]
        for off in range(1, n_ply):
            peer = lax.rem(ply + off, n_ply)
            copy = pltpu.make_async_remote_copy(
                src_ref=half.at[s], dst_ref=tot.at[s, peer],
                send_sem=qs_sem.at[s, off], recv_sem=qr_sem.at[s, peer],
                device_id=(peer, tile), device_id_type=MESH,
            )
            copy.wait_recv()
            copy.wait_send()
        total = tot[s, 0]
        for j in range(1, n_ply):
            total = total + tot[s, j]
        root = jnp.sqrt(jnp.full((8, 128), jnp.sum(total)) / sites + epsilon)
        rec_out[s] = root[0, 0]

    ins[0].wait()
    send(P0, pb.at[0])
    for copy in ins[1:4]:
        copy.wait()
    for p in range(planes):
        mb[0, p] = mobility_of(tb[0, p], cb[0, p], kb[p])
    send(MOB[0], mb.at[0])
    for copy in ins[4:]:
        copy.wait()
    for p in range(planes):
        wet = flags[0, p].astype(jnp.float32)
        inlet = flags[1, p].astype(jnp.float32)
        loose = wet * (1.0 - inlet) * (1.0 - flags[2, p].astype(jnp.float32))
        fill[p] = wet
        free[p] = loose
        fixed[p] = jnp.where(loose > 0, 0.0, inlet)
        fills[0, p] = jnp.where(last_row, 0.0, up(wet, 0))
        fills[1, p] = jnp.where(first_row, 0.0, down(wet, 0))
        fills[2, p] = jnp.where(last_lane, 0.0, up(wet, 1))
        fills[3, p] = jnp.where(first_lane, 0.0, down(wet, 1))

    before = P0
    for s in range(STEPS):
        for p in range(planes):
            m = mb[s, p]
            if p:
                fz[p] = face(mb[s, p - 1], m)
            a = jnp.where(last_row, 0.0, face(m, up(m, 0)))
            fy[0, p] = a
            fy[1, p] = jnp.where(first_row, 0.0, down(a, 0))
            b = jnp.where(last_lane, 0.0, face(m, up(m, 1)))
            fx[0, p] = b
            fx[1, p] = jnp.where(first_lane, 0.0, down(b, 1))

        def inside(x):
            for p in range(planes):
                v = x[p]
                total = fx[0, p] * up(v, 1) + fx[1, p] * down(v, 1)
                total += fy[0, p] * up(v, 0) + fy[1, p] * down(v, 0)
                if p:
                    total += fz[p] * x[p - 1]
                if p < planes - 1:
                    total += fz[p + 1] * x[p + 1]
                acc[p] = total

        inside(pb.at[s * SWEEPS])
        landed(MOB[s], mb.at[s], (2, 3, 0, 1))
        fz[0] = face(mb[s, 0], low_plane(MOB[s]))
        fz[planes] = face(mb[s, planes - 1], high_plane(MOB[s]))
        for p in range(planes):
            beside = face(mb[s, p], edge_rows(MOB[s], p))
            fh[p] = beside
            total = fz[p] + fz[p + 1] + fy[0, p] + fy[1, p] + beside + fx[0, p] + fx[1, p]
            diag[p] = total
            moving = free[p] > 0
            inv[p] = jnp.where(moving, 1.0 / jnp.where(moving, total, 1.0), 0.0)

        order = list(range(1, planes - 1))
        for k in range(SWEEPS):
            old, new = pb.at[s * SWEEPS + k], pb.at[s * SWEEPS + k + 1]
            if s == 0 or k:
                landed(before, old, (2, 3))

            def finish(p):
                total = acc[p] + fh[p] * edge_rows(before, p)
                if p == 0:
                    total += fz[0] * low_plane(before)
                if p == planes - 1:
                    total += fz[planes] * high_plane(before)
                new[p] = total * inv[p] + fixed[p]

            for p in order:
                finish(p)
            if planes > 1:
                if s == 0 or k:
                    landed(before, old, (1,))
                finish(0)
                send(PRESS[s][k], new, (0,))
                if s == 0 or k:
                    landed(before, old, (0,))
                finish(planes - 1)
                send(PRESS[s][k], new, (1, 2, 3))
            else:
                if s == 0 or k:
                    landed(before, old, (0, 1))
                finish(0)
                send(PRESS[s][k], new)
            if k == 0:
                send(WARM[s], tb.at[s])
            if k == 1:
                send(CURE[s], cb.at[s])
            if k == 2 and s == 0:
                send(FILL, fill)
            if k == 1 and s:
                reduce_mid(s - 1)
            inside(new)
            before = PRESS[s][k]

        now = s * SWEEPS + SWEEPS
        if s == STEPS - 1:
            pltpu.make_async_copy(pb.at[now], p_out, out_sem.at[0]).start()
        landed(WARM[s], tb.at[s], (0, 1, 2, 3))
        landed(CURE[s], cb.at[s], (0, 1, 2, 3))
        if s == 0:
            landed(FILL, fill, (0, 1, 2, 3))

        def stream(p, f, press, warm, cure, wet):
            q = jnp.maximum(f * (press - pb[now, p]), 0.0) * wet
            dt = warm - tb[s, p]
            return (q + diffusion_coefficient * wet) * dt, q * (cure - cb[s, p])

        gained = []
        for p in range(planes):
            v, t, c = pb[now, p], tb[s, p], cb[s, p]
            speed = arrhenius_prefactor * jnp.exp(arrhenius_barrier * (1.0 - 1.0 / t)) * (1.0 - c)
            dt, dc = released_enthalpy * speed, speed
            for n, (move, axis, f) in enumerate(
                [(up, 0, fy[0, p]), (down, 0, fy[1, p]), (up, 1, fx[0, p]), (down, 1, fx[1, p])]
            ):
                a, b = stream(p, f, move(v, axis), move(t, axis), move(c, axis), fills[n, p])
                dt, dc = dt + a, dc + b
            for q, f in [(p - 1, fz[p]), (p + 1, fz[p + 1])]:
                if 0 <= q < planes:
                    a, b = stream(p, f, pb[now, q], tb[s, q], cb[s, q], fill[q])
                    dt, dc = dt + a, dc + b
            tb[s + 1, p] = dt
            cb[s + 1, p] = dc

        landed(before, pb.at[now], (2, 3, 0, 1))
        squares = jnp.zeros((rows, width), jnp.float32)
        for p in range(planes):
            total = acc[p] + fh[p] * edge_rows(before, p)
            if p == 0:
                total += fz[0] * low_plane(before)
            if p == planes - 1:
                total += fz[planes] * high_plane(before)
            off = free[p] * (total - diag[p] * pb[now, p])
            squares += off * off
        small = jnp.zeros((8, 128), jnp.float32)
        for r in range(0, rows, 8):
            for l in range(0, width, 128):
                small += squares[r:r + 8, l:l + 128]
        part[s] = small
        if s == STEPS - 1:
            reduce_send(s)
        for p in range(planes):
            dt, dc = tb[s + 1, p], cb[s + 1, p]
            ways = [(fh[p], edge_rows(before, p), edge_rows(WARM[s], p), edge_rows(CURE[s], p),
                     edge_rows(FILL, p))]
            if p == 0:
                ways.append((fz[0], low_plane(before), low_plane(WARM[s]), low_plane(CURE[s]),
                             low_plane(FILL)))
            if p == planes - 1:
                ways.append((fz[planes], high_plane(before), high_plane(WARM[s]),
                             high_plane(CURE[s]), high_plane(FILL)))
            for way in ways:
                a, b = stream(p, *way)
                dt, dc = dt + a, dc + b
            share = fill[p] * clock_step_size
            t = tb[s, p] + share * dt
            c = cb[s, p] + share * dc
            tb[s + 1, p] = t
            cb[s + 1, p] = c
            if s < STEPS - 1:
                mb[s + 1, p] = mobility_of(t, c, kb[p])
        if s < STEPS - 1:
            send(MOB[s + 1], mb.at[s + 1])
            reduce_send(s)

    outs = [
        pltpu.make_async_copy(pb.at[STEPS * SWEEPS], p_out, out_sem.at[0]),
        pltpu.make_async_copy(tb.at[STEPS], t_out, out_sem.at[1]),
        pltpu.make_async_copy(cb.at[STEPS], c_out, out_sem.at[2]),
    ]
    outs[1].start()
    outs[2].start()
    reduce_mid(STEPS - 1)
    for s in range(STEPS - 1):
        reduce_end(s)
    for m, src in sources.items():
        sent(m, src)
    reduce_end(STEPS - 1)
    for copy in outs:
        copy.wait()


def per_device(n_ply, n_tile, *fields):
    shape = fields[0].shape
    planes, rows, width = shape
    real = jnp.float32

    def block(*lead):
        return pltpu.VMEM((*lead, *shape), real)

    dma = pltpu.SemaphoreType.DMA
    scratch = [
        block(STEPS + 1), block(STEPS + 1), block(STEPS * SWEEPS + 1), block(STEPS), block(),
        pltpu.VMEM((3, *shape), jnp.int32), block(), block(), block(), block(4),
        pltpu.VMEM((planes + 1, rows, width), real), block(2), block(2), block(), block(), block(),
        block(), pltpu.VMEM((STEPS, 8, 128), real),
        pltpu.VMEM((MESSAGES, 2, rows, width), real), block(MESSAGES),
        pltpu.VMEM((STEPS, n_tile, 8, 128), real), pltpu.VMEM((STEPS, 8, 128), real),
        pltpu.VMEM((STEPS, n_ply, 8, 128), real),
        dma((7,)), dma((3,)), dma((MESSAGES, 4)), dma((MESSAGES, 4)),
        dma((STEPS, n_tile)), dma((STEPS, n_tile)), dma((STEPS, n_ply)), dma((STEPS, n_ply)),
    ]
    out = jax.ShapeDtypeStruct(shape, real)
    anywhere = pl.BlockSpec(memory_space=pl.ANY)
    return pl.pallas_call(
        functools.partial(kernel, n_ply, n_tile),
        out_shape=(out, out, out, jax.ShapeDtypeStruct((STEPS,), real)),
        in_specs=[anywhere] * 7,
        out_specs=(anywhere, anywhere, anywhere, pl.BlockSpec(memory_space=pltpu.SMEM)),
        scratch_shapes=scratch,
        compiler_params=pltpu.CompilerParams(
            collective_id=0, has_side_effects=True, vmem_limit_bytes=24 * 1024 * 1024
        ),
    )(*fields)


def solution(mesh):
    spec = P("ply", "tile", None)
    return jax.shard_map(
        functools.partial(per_device, mesh.shape["ply"], mesh.shape["tile"]),
        mesh=mesh,
        in_specs=(spec,) * 7,
        out_specs=(spec, spec, spec, P()),
        check_vma=False,
    )
```

```python
import functools

import jax
import jax.numpy as jnp
from jax import lax
from jax.experimental import pallas as pl
from jax.experimental.pallas import tpu as pltpu
from jax.sharding import PartitionSpec as P

STEPS = 2
SWEEPS = 4

fluidity_barrier = 4.0
fluidity_gelation_coefficient = 2.0
arrhenius_prefactor = 0.2
arrhenius_barrier = 8.0
released_enthalpy = 0.3
diffusion_coefficient = 0.1
clock_step_size = 0.5
epsilon = 1e-06

MESH = pl.DeviceIdType.MESH
MOB = STEPS * SWEEPS + 1
WARM, CURE = MOB + STEPS, MOB + 2 * STEPS
FILL = MOB + 3 * STEPS
MESSAGES = FILL + 1


def mobility_of(warmth, cure, preform):
    return preform * jnp.exp(
        -(fluidity_barrier * (1.0 / warmth - 1.0) + fluidity_gelation_coefficient * cure)
    )


def face(m, k):
    denom = m + k
    return 2.0 * m * k / jnp.where(denom > 0, denom, 1.0)


def kernel(
    n_ply, n_tile,
    t_in, c_in, p_in, k_in, w_in, i_in, o_in,
    t_out, c_out, p_out, rec_out,
    tb, cb, pb, mb, kb, flags, fill, free, fixed, fills, fz, fy, fx, fh, diag, inv, acc, part,
    hp, hr, red, half, tot,
    in_sem, out_sem, send_sem, recv_sem, rs_sem, rr_sem, qs_sem, qr_sem,
):
    planes, rows, width = p_in.shape
    ply, tile = lax.axis_index("ply"), lax.axis_index("tile")
    sites = planes * rows * width * n_ply * n_tile

    ins = [
        pltpu.make_async_copy(src, dst, in_sem.at[n])
        for n, (src, dst) in enumerate(
            [(p_in, pb.at[0]), (t_in, tb.at[0]), (c_in, cb.at[0]), (k_in, kb),
             (w_in, flags.at[0]), (i_in, flags.at[1]), (o_in, flags.at[2])]
        )
    ]
    for copy in ins:
        copy.start()

    barrier = pltpu.get_barrier_semaphore()
    for off in range(1, n_ply):
        pl.semaphore_signal(
            barrier, inc=1, device_id=(lax.rem(ply + off, n_ply), tile), device_id_type=MESH
        )

    def greet(off, carry):
        pl.semaphore_signal(
            barrier, inc=1, device_id=(ply, lax.rem(tile + off, n_tile)), device_id_type=MESH
        )
        return carry

    lax.fori_loop(1, n_tile, greet, 0)
    pl.semaphore_wait(barrier, n_ply + n_tile - 2)

    has = [ply < n_ply - 1, ply > 0, tile < n_tile - 1, tile > 0]

    def message(m, src, d):
        if d < 2:
            edge = 0 if d == 0 else planes - 1
            a, b = src.at[edge], hp.at[m, 1 - d]
            where = (ply - 1 if d == 0 else ply + 1, tile)
        else:
            lo, hi = pl.ds(0, 1), pl.ds(rows - 1, 1)
            a = src.at[:, lo if d == 2 else hi]
            b = hr.at[m, :, hi if d == 2 else lo]
            where = (ply, tile - 1 if d == 2 else tile + 1)
        return pltpu.make_async_remote_copy(
            src_ref=a, dst_ref=b, send_sem=send_sem.at[m, d], recv_sem=recv_sem.at[m, d],
            device_id=where, device_id_type=MESH,
        )

    opposite = [1, 0, 3, 2]

    def send(m, src, ds=(0, 1, 2, 3)):
        for d in ds:
            pl.when(has[opposite[d]])(lambda d=d: message(m, src, d).start())

    def landed(m, src, ds):
        for d in ds:
            pl.when(has[d])(lambda d=d: message(m, src, d).wait_recv())

    def sent(m, src):
        for d in range(4):
            pl.when(has[opposite[d]])(lambda d=d: message(m, src, d).wait_send())

    row = lax.broadcasted_iota(jnp.int32, (rows, width), 0)
    lane = lax.broadcasted_iota(jnp.int32, (rows, width), 1)
    first_row, last_row = row == 0, row == rows - 1
    edge_row = (first_row & (tile > 0)) | (last_row & (tile < n_tile - 1))
    first_lane, last_lane = lane == 0, lane == width - 1

    def up(x, axis):
        return pltpu.roll(x, x.shape[axis] - 1, axis)

    def down(x, axis):
        return pltpu.roll(x, 1, axis)

    def low_plane(m):
        return jnp.where(ply > 0, hp[m, 0], 0.0)

    def high_plane(m):
        return jnp.where(ply < n_ply - 1, hp[m, 1], 0.0)

    def edge_rows(m, p):
        return jnp.where(edge_row, hr[m, p], 0.0)

    def reduce_send():
        def body(off, carry):
            pltpu.make_async_remote_copy(
                src_ref=part, dst_ref=red.at[tile],
                send_sem=rs_sem.at[off], recv_sem=rr_sem.at[tile],
                device_id=(ply, lax.rem(tile + off, n_tile)), device_id_type=MESH,
            ).start()
            return carry

        lax.fori_loop(1, n_tile, body, 0)

    def reduce_mid():
        def body(off, total):
            peer = lax.rem(tile + off, n_tile)
            copy = pltpu.make_async_remote_copy(
                src_ref=part, dst_ref=red.at[peer],
                send_sem=rs_sem.at[off], recv_sem=rr_sem.at[peer],
                device_id=(ply, peer), device_id_type=MESH,
            )
            copy.wait_recv()
            copy.wait_send()
            return total + red[peer]

        half[...] = lax.fori_loop(1, n_tile, body, part[...])
        for off in range(1, n_ply):
            pltpu.make_async_remote_copy(
                src_ref=half, dst_ref=tot.at[ply],
                send_sem=qs_sem.at[off], recv_sem=qr_sem.at[ply],
                device_id=(lax.rem(ply + off, n_ply), tile), device_id_type=MESH,
            ).start()

    def reduce_end():
        tot[ply] = half[...]
        for off in range(1, n_ply):
            peer = lax.rem(ply + off, n_ply)
            copy = pltpu.make_async_remote_copy(
                src_ref=half, dst_ref=tot.at[peer],
                send_sem=qs_sem.at[off], recv_sem=qr_sem.at[peer],
                device_id=(peer, tile), device_id_type=MESH,
            )
            copy.wait_recv()
            copy.wait_send()
        total = tot[0]
        for j in range(1, n_ply):
            total = total + tot[j]
        for s in range(STEPS):
            root = jnp.sqrt(jnp.full((8, 128), jnp.sum(total[s])) / sites + epsilon)
            rec_out[s] = root[0, 0]

    ins[0].wait()
    send(0, pb.at[0])
    for copy in ins[1:4]:
        copy.wait()
    for p in range(planes):
        mb[0, p] = mobility_of(tb[0, p], cb[0, p], kb[p])
    send(MOB, mb.at[0])
    for copy in ins[4:]:
        copy.wait()
    for p in range(planes):
        wet = flags[0, p].astype(jnp.float32)
        inlet = flags[1, p].astype(jnp.float32)
        loose = wet * (1.0 - inlet) * (1.0 - flags[2, p].astype(jnp.float32))
        fill[p] = wet
        free[p] = loose
        fixed[p] = jnp.where(loose > 0, 0.0, inlet)
        fills[0, p] = jnp.where(last_row, 0.0, up(wet, 0))
        fills[1, p] = jnp.where(first_row, 0.0, down(wet, 0))
        fills[2, p] = jnp.where(last_lane, 0.0, up(wet, 1))
        fills[3, p] = jnp.where(first_lane, 0.0, down(wet, 1))

    def time_step(s, carry):
        for p in range(planes):
            m = mb[s, p]
            if p:
                fz[p] = face(mb[s, p - 1], m)
            a = jnp.where(last_row, 0.0, face(m, up(m, 0)))
            fy[0, p] = a
            fy[1, p] = jnp.where(first_row, 0.0, down(a, 0))
            b = jnp.where(last_lane, 0.0, face(m, up(m, 1)))
            fx[0, p] = b
            fx[1, p] = jnp.where(first_lane, 0.0, down(b, 1))
        landed(MOB + s, mb.at[s], (2, 3, 0, 1))
        fz[0] = face(mb[s, 0], low_plane(MOB + s))
        fz[planes] = face(mb[s, planes - 1], high_plane(MOB + s))
        for p in range(planes):
            beside = face(mb[s, p], edge_rows(MOB + s, p))
            fh[p] = beside
            total = fz[p] + fz[p + 1] + fy[0, p] + fy[1, p] + beside + fx[0, p] + fx[1, p]
            diag[p] = total
            moving = free[p] > 0
            inv[p] = jnp.where(moving, 1.0 / jnp.where(moving, total, 1.0), 0.0)

        def inside(x):
            for p in range(planes):
                v = x[p]
                total = fx[0, p] * up(v, 1) + fx[1, p] * down(v, 1)
                total += fy[0, p] * up(v, 0) + fy[1, p] * down(v, 0)
                if p:
                    total += fz[p] * x[p - 1]
                if p < planes - 1:
                    total += fz[p + 1] * x[p + 1]
                acc[p] = total

        def arrive(j, ds, fresh):
            for d in ds:
                pl.when(has[d] & fresh)(lambda d=d: message(j, pb.at[j], d).wait_recv())

        def sweep(k, carry):
            j = s * SWEEPS + k
            old, new = pb.at[j], pb.at[j + 1]
            fresh = (s == 0) | (k > 0)
            inside(old)
            arrive(j, (2, 3), fresh)

            def finish(p):
                total = acc[p] + fh[p] * edge_rows(j, p)
                if p == 0:
                    total += fz[0] * low_plane(j)
                if p == planes - 1:
                    total += fz[planes] * high_plane(j)
                new[p] = total * inv[p] + fixed[p]

            for p in range(1, planes - 1):
                finish(p)
            if planes > 1:
                arrive(j, (1,), fresh)
                finish(0)
                send(j + 1, new, (0,))
                arrive(j, (0,), fresh)
                finish(planes - 1)
                send(j + 1, new, (1, 2, 3))
            else:
                arrive(j, (0, 1), fresh)
                finish(0)
                send(j + 1, new)
            pl.when(k == 0)(lambda: send(WARM + s, tb.at[s]))
            pl.when(k == 1)(lambda: send(CURE + s, cb.at[s]))
            pl.when((k == 2) & (s == 0))(lambda: send(FILL, fill))
            return carry

        lax.fori_loop(0, SWEEPS, sweep, 0)

        now = (s + 1) * SWEEPS
        last = s == STEPS - 1
        inside(pb.at[now])
        landed(WARM + s, tb.at[s], (0, 1, 2, 3))
        landed(CURE + s, cb.at[s], (0, 1, 2, 3))

        @pl.when(s == 0)
        def _():
            landed(FILL, fill, (0, 1, 2, 3))

        def stream(p, f, press, warm, cure, wet):
            q = jnp.maximum(f * (press - pb[now, p]), 0.0) * wet
            dt = warm - tb[s, p]
            return (q + diffusion_coefficient * wet) * dt, q * (cure - cb[s, p])

        for p in range(planes):
            v, t, c = pb[now, p], tb[s, p], cb[s, p]
            speed = arrhenius_prefactor * jnp.exp(arrhenius_barrier * (1.0 - 1.0 / t)) * (1.0 - c)
            dt, dc = released_enthalpy * speed, speed
            for n, (move, axis, f) in enumerate(
                [(up, 0, fy[0, p]), (down, 0, fy[1, p]), (up, 1, fx[0, p]), (down, 1, fx[1, p])]
            ):
                a, b = stream(p, f, move(v, axis), move(t, axis), move(c, axis), fills[n, p])
                dt, dc = dt + a, dc + b
            for q, f in [(p - 1, fz[p]), (p + 1, fz[p + 1])]:
                if 0 <= q < planes:
                    a, b = stream(p, f, pb[now, q], tb[s, q], cb[s, q], fill[q])
                    dt, dc = dt + a, dc + b
            tb[s + 1, p] = dt
            cb[s + 1, p] = dc

        landed(now, pb.at[now], (2, 3, 0, 1))
        squares = jnp.zeros((rows, width), jnp.float32)
        for p in range(planes):
            total = acc[p] + fh[p] * edge_rows(now, p)
            if p == 0:
                total += fz[0] * low_plane(now)
            if p == planes - 1:
                total += fz[planes] * high_plane(now)
            off = free[p] * (total - diag[p] * pb[now, p])
            squares += off * off
        small = jnp.zeros((8, 128), jnp.float32)
        for r in range(0, rows, 8):
            for l in range(0, width, 128):
                small += squares[r:r + 8, l:l + 128]
        part[s] = small
        pl.when(last)(reduce_send)
        for p in range(planes):
            dt, dc = tb[s + 1, p], cb[s + 1, p]
            ways = [(fh[p], edge_rows(now, p), edge_rows(WARM + s, p), edge_rows(CURE + s, p),
                     edge_rows(FILL, p))]
            if p == 0:
                ways.append((fz[0], low_plane(now), low_plane(WARM + s), low_plane(CURE + s),
                             low_plane(FILL)))
            if p == planes - 1:
                ways.append((fz[planes], high_plane(now), high_plane(WARM + s),
                             high_plane(CURE + s), high_plane(FILL)))
            for way in ways:
                a, b = stream(p, *way)
                dt, dc = dt + a, dc + b
            share = fill[p] * clock_step_size
            t = tb[s, p] + share * dt
            c = cb[s, p] + share * dc
            tb[s + 1, p] = t
            cb[s + 1, p] = c
            mb[s + 1, p] = mobility_of(t, c, kb[p])
        pl.when(s < STEPS - 1)(lambda: send(MOB + s + 1, mb.at[s + 1]))
        return carry

    lax.fori_loop(0, STEPS, time_step, 0)

    outs = [
        pltpu.make_async_copy(pb.at[STEPS * SWEEPS], p_out, out_sem.at[0]),
        pltpu.make_async_copy(tb.at[STEPS], t_out, out_sem.at[1]),
        pltpu.make_async_copy(cb.at[STEPS], c_out, out_sem.at[2]),
    ]
    for copy in outs:
        copy.start()
    reduce_mid()

    def drain(m, carry):
        sent(m, pb.at[0])
        return carry

    lax.fori_loop(0, MESSAGES, drain, 0)
    reduce_end()
    for copy in outs:
        copy.wait()


def per_device(n_ply, n_tile, *fields):
    shape = fields[0].shape
    planes, rows, width = shape
    real = jnp.float32

    def block(*lead):
        return pltpu.VMEM((*lead, *shape), real)

    dma = pltpu.SemaphoreType.DMA
    scratch = [
        block(STEPS + 1), block(STEPS + 1), block(STEPS * SWEEPS + 1), block(STEPS + 1), block(),
        pltpu.VMEM((3, *shape), jnp.int32), block(), block(), block(), block(4),
        pltpu.VMEM((planes + 1, rows, width), real), block(2), block(2), block(), block(), block(),
        block(), pltpu.VMEM((STEPS, 8, 128), real),
        pltpu.VMEM((MESSAGES, 2, rows, width), real), block(MESSAGES),
        pltpu.VMEM((n_tile, STEPS, 8, 128), real), pltpu.VMEM((STEPS, 8, 128), real),
        pltpu.VMEM((n_ply, STEPS, 8, 128), real),
        dma((7,)), dma((3,)), dma((MESSAGES, 4)), dma((MESSAGES, 4)),
        dma((n_tile,)), dma((n_tile,)), dma((n_ply,)), dma((n_ply,)),
    ]
    out = jax.ShapeDtypeStruct(shape, real)
    anywhere = pl.BlockSpec(memory_space=pl.ANY)
    return pl.pallas_call(
        functools.partial(kernel, n_ply, n_tile),
        out_shape=(out, out, out, jax.ShapeDtypeStruct((STEPS,), real)),
        in_specs=[anywhere] * 7,
        out_specs=(anywhere, anywhere, anywhere, pl.BlockSpec(memory_space=pltpu.SMEM)),
        scratch_shapes=scratch,
        compiler_params=pltpu.CompilerParams(
            collective_id=0, has_side_effects=True, vmem_limit_bytes=60 * 1024 * 1024
        ),
    )(*fields)


def solution(mesh):
    spec = P("ply", "tile", None)
    return jax.shard_map(
        functools.partial(per_device, mesh.shape["ply"], mesh.shape["tile"]),
        mesh=mesh,
        in_specs=(spec,) * 7,
        out_specs=(spec, spec, spec, P()),
        check_vma=False,
    )
```

```python
import functools

import jax
import jax.numpy as jnp
from jax import lax
from jax.experimental import pallas as pl
from jax.experimental.pallas import tpu as pltpu
from jax.sharding import PartitionSpec as P

STEPS = 2
SWEEPS = 4

fluidity_barrier = 4.0
fluidity_gelation_coefficient = 2.0
arrhenius_prefactor = 0.2
arrhenius_barrier = 8.0
released_enthalpy = 0.3
diffusion_coefficient = 0.1
clock_step_size = 0.5
epsilon = 1e-06

MESH = pl.DeviceIdType.MESH
MOB = STEPS * SWEEPS + 1
WARM, CURE = MOB + STEPS, MOB + 2 * STEPS
FILL = MOB + 3 * STEPS
MESSAGES = FILL + 1


def mobility_of(warmth, cure, preform):
    return preform * jnp.exp(
        -(fluidity_barrier * (1.0 / warmth - 1.0) + fluidity_gelation_coefficient * cure)
    )


def face(m, k):
    denom = m + k
    return 2.0 * m * k / jnp.where(denom > 0, denom, 1.0)


def kernel(
    n_ply, n_tile,
    t_in, c_in, p_in, k_in, w_in, i_in, o_in,
    t_out, c_out, p_out, rec_out,
    tb, cb, pb, mb, kb, flags, fill, free, fixed, fills, fz, fy, fx, fh, diag, inv, acc, part,
    hp, hr, red, half, tot,
    in_sem, out_sem, send_sem, recv_sem, rs_sem, rr_sem, qs_sem, qr_sem,
):
    planes, rows, width = p_in.shape
    ply, tile = lax.axis_index("ply"), lax.axis_index("tile")
    sites = planes * rows * width * n_ply * n_tile

    ins = [
        pltpu.make_async_copy(src, dst, in_sem.at[n])
        for n, (src, dst) in enumerate(
            [(p_in, pb.at[0]), (t_in, tb.at[0]), (c_in, cb.at[0]), (k_in, kb),
             (w_in, flags.at[0]), (i_in, flags.at[1]), (o_in, flags.at[2])]
        )
    ]
    for copy in ins:
        copy.start()

    barrier = pltpu.get_barrier_semaphore()
    for off in range(1, n_ply):
        pl.semaphore_signal(
            barrier, inc=1, device_id=(lax.rem(ply + off, n_ply), tile), device_id_type=MESH
        )

    def greet(off, carry):
        pl.semaphore_signal(
            barrier, inc=1, device_id=(ply, lax.rem(tile + off, n_tile)), device_id_type=MESH
        )
        return carry

    lax.fori_loop(1, n_tile, greet, 0)
    pl.semaphore_wait(barrier, n_ply + n_tile - 2)

    has = [ply < n_ply - 1, ply > 0, tile < n_tile - 1, tile > 0]

    def message(m, src, d):
        if d < 2:
            edge = 0 if d == 0 else planes - 1
            a, b = src.at[edge], hp.at[m, 1 - d]
            where = (ply - 1 if d == 0 else ply + 1, tile)
        else:
            lo, hi = pl.ds(0, 1), pl.ds(rows - 1, 1)
            a = src.at[:, lo if d == 2 else hi]
            b = hr.at[m, :, hi if d == 2 else lo]
            where = (ply, tile - 1 if d == 2 else tile + 1)
        return pltpu.make_async_remote_copy(
            src_ref=a, dst_ref=b, send_sem=send_sem.at[m, d], recv_sem=recv_sem.at[m, d],
            device_id=where, device_id_type=MESH,
        )

    opposite = [1, 0, 3, 2]

    def send(m, src, ds=(0, 1, 2, 3)):
        for d in ds:
            pl.when(has[opposite[d]])(lambda d=d: message(m, src, d).start())

    def landed(m, src, ds):
        for d in ds:
            pl.when(has[d])(lambda d=d: message(m, src, d).wait_recv())

    def sent(m, src):
        for d in range(4):
            pl.when(has[opposite[d]])(lambda d=d: message(m, src, d).wait_send())

    row = lax.broadcasted_iota(jnp.int32, (rows, width), 0)
    lane = lax.broadcasted_iota(jnp.int32, (rows, width), 1)
    first_row, last_row = row == 0, row == rows - 1
    edge_row = (first_row & (tile > 0)) | (last_row & (tile < n_tile - 1))
    first_lane, last_lane = lane == 0, lane == width - 1

    def up(x, axis):
        return pltpu.roll(x, x.shape[axis] - 1, axis)

    def down(x, axis):
        return pltpu.roll(x, 1, axis)

    def low_plane(m):
        return jnp.where(ply > 0, hp[m, 0], 0.0)

    def high_plane(m):
        return jnp.where(ply < n_ply - 1, hp[m, 1], 0.0)

    def edge_rows(m, p):
        return jnp.where(edge_row, hr[m, p], 0.0)

    def reduce_send():
        def body(off, carry):
            pltpu.make_async_remote_copy(
                src_ref=part, dst_ref=red.at[tile],
                send_sem=rs_sem.at[off], recv_sem=rr_sem.at[tile],
                device_id=(ply, lax.rem(tile + off, n_tile)), device_id_type=MESH,
            ).start()
            return carry

        lax.fori_loop(1, n_tile, body, 0)

    def reduce_mid():
        def body(off, total):
            peer = lax.rem(tile + off, n_tile)
            copy = pltpu.make_async_remote_copy(
                src_ref=part, dst_ref=red.at[peer],
                send_sem=rs_sem.at[off], recv_sem=rr_sem.at[peer],
                device_id=(ply, peer), device_id_type=MESH,
            )
            copy.wait_recv()
            copy.wait_send()
            return total + red[peer]

        half[...] = lax.fori_loop(1, n_tile, body, part[...])
        for off in range(1, n_ply):
            pltpu.make_async_remote_copy(
                src_ref=half, dst_ref=tot.at[ply],
                send_sem=qs_sem.at[off], recv_sem=qr_sem.at[ply],
                device_id=(lax.rem(ply + off, n_ply), tile), device_id_type=MESH,
            ).start()

    def reduce_end():
        tot[ply] = half[...]
        for off in range(1, n_ply):
            peer = lax.rem(ply + off, n_ply)
            copy = pltpu.make_async_remote_copy(
                src_ref=half, dst_ref=tot.at[peer],
                send_sem=qs_sem.at[off], recv_sem=qr_sem.at[peer],
                device_id=(peer, tile), device_id_type=MESH,
            )
            copy.wait_recv()
            copy.wait_send()
        total = tot[0]
        for j in range(1, n_ply):
            total = total + tot[j]
        for s in range(STEPS):
            root = jnp.sqrt(jnp.full((8, 128), jnp.sum(total[s])) / sites + epsilon)
            rec_out[s] = root[0, 0]

    ins[0].wait()
    send(0, pb.at[0])
    for copy in ins[1:4]:
        copy.wait()
    for p in range(planes):
        mb[0, p] = mobility_of(tb[0, p], cb[0, p], kb[p])
    send(MOB, mb.at[0])
    for copy in ins[4:]:
        copy.wait()
    for p in range(planes):
        wet = flags[0, p].astype(jnp.float32)
        inlet = flags[1, p].astype(jnp.float32)
        loose = wet * (1.0 - inlet) * (1.0 - flags[2, p].astype(jnp.float32))
        fill[p] = wet
        free[p] = loose
        fixed[p] = jnp.where(loose > 0, 0.0, inlet)
        fills[0, p] = jnp.where(last_row, 0.0, up(wet, 0))
        fills[1, p] = jnp.where(first_row, 0.0, down(wet, 0))
        fills[2, p] = jnp.where(last_lane, 0.0, up(wet, 1))
        fills[3, p] = jnp.where(first_lane, 0.0, down(wet, 1))

    def time_step(s, carry):
        for p in range(planes):
            m = mb[s, p]
            if p:
                fz[p] = face(mb[s, p - 1], m)
            a = jnp.where(last_row, 0.0, face(m, up(m, 0)))
            fy[0, p] = a
            fy[1, p] = jnp.where(first_row, 0.0, down(a, 0))
            b = jnp.where(last_lane, 0.0, face(m, up(m, 1)))
            fx[0, p] = b
            fx[1, p] = jnp.where(first_lane, 0.0, down(b, 1))
        landed(MOB + s, mb.at[s], (2, 3, 0, 1))
        fz[0] = face(mb[s, 0], low_plane(MOB + s))
        fz[planes] = face(mb[s, planes - 1], high_plane(MOB + s))
        for p in range(planes):
            beside = face(mb[s, p], edge_rows(MOB + s, p))
            fh[p] = beside
            total = fz[p] + fz[p + 1] + fy[0, p] + fy[1, p] + beside + fx[0, p] + fx[1, p]
            diag[p] = total
            moving = free[p] > 0
            inv[p] = jnp.where(moving, 1.0 / jnp.where(moving, total, 1.0), 0.0)

        def inside(x):
            for p in range(planes):
                v = x[p]
                total = fx[0, p] * up(v, 1) + fx[1, p] * down(v, 1)
                total += fy[0, p] * up(v, 0) + fy[1, p] * down(v, 0)
                if p:
                    total += fz[p] * x[p - 1]
                if p < planes - 1:
                    total += fz[p + 1] * x[p + 1]
                acc[p] = total

        def arrive(j, ds, fresh):
            for d in ds:
                pl.when(has[d] & fresh)(lambda d=d: message(j, pb.at[j], d).wait_recv())

        def sweep(k, carry):
            j = s * SWEEPS + k
            old, new = pb.at[j], pb.at[j + 1]
            fresh = (s == 0) | (k > 0)
            inside(old)
            arrive(j, (2, 3), fresh)

            def finish(p):
                total = acc[p] + fh[p] * edge_rows(j, p)
                if p == 0:
                    total += fz[0] * low_plane(j)
                if p == planes - 1:
                    total += fz[planes] * high_plane(j)
                new[p] = total * inv[p] + fixed[p]

            for p in range(1, planes - 1):
                finish(p)
            if planes > 1:
                arrive(j, (1,), fresh)
                finish(0)
                send(j + 1, new, (0,))
                arrive(j, (0,), fresh)
                finish(planes - 1)
                send(j + 1, new, (1, 2, 3))
            else:
                arrive(j, (0, 1), fresh)
                finish(0)
                send(j + 1, new)
            pl.when(k == 0)(lambda: send(WARM + s, tb.at[s]))
            pl.when(k == 1)(lambda: send(CURE + s, cb.at[s]))
            pl.when((k == 2) & (s == 0))(lambda: send(FILL, fill))
            return carry

        lax.fori_loop(0, SWEEPS, sweep, 0)

        now = (s + 1) * SWEEPS
        last = s == STEPS - 1
        inside(pb.at[now])
        landed(WARM + s, tb.at[s], (0, 1, 2, 3))
        landed(CURE + s, cb.at[s], (0, 1, 2, 3))

        @pl.when(s == 0)
        def _():
            landed(FILL, fill, (0, 1, 2, 3))

        def stream(p, f, press, warm, cure, wet):
            q = jnp.maximum(f * (press - pb[now, p]), 0.0) * wet
            dt = warm - tb[s, p]
            return (q + diffusion_coefficient * wet) * dt, q * (cure - cb[s, p])

        for p in range(planes):
            v, t, c = pb[now, p], tb[s, p], cb[s, p]
            speed = arrhenius_prefactor * jnp.exp(arrhenius_barrier * (1.0 - 1.0 / t)) * (1.0 - c)
            dt, dc = released_enthalpy * speed, speed
            for n, (move, axis, f) in enumerate(
                [(up, 0, fy[0, p]), (down, 0, fy[1, p]), (up, 1, fx[0, p]), (down, 1, fx[1, p])]
            ):
                a, b = stream(p, f, move(v, axis), move(t, axis), move(c, axis), fills[n, p])
                dt, dc = dt + a, dc + b
            for q, f in [(p - 1, fz[p]), (p + 1, fz[p + 1])]:
                if 0 <= q < planes:
                    a, b = stream(p, f, pb[now, q], tb[s, q], cb[s, q], fill[q])
                    dt, dc = dt + a, dc + b
            tb[s + 1, p] = dt
            cb[s + 1, p] = dc

        landed(now, pb.at[now], (2, 3, 0, 1))
        squares = jnp.zeros((rows, width), jnp.float32)
        for p in range(planes):
            total = acc[p] + fh[p] * edge_rows(now, p)
            if p == 0:
                total += fz[0] * low_plane(now)
            if p == planes - 1:
                total += fz[planes] * high_plane(now)
            off = free[p] * (total - diag[p] * pb[now, p])
            squares += off * off
        small = jnp.zeros((8, 128), jnp.float32)
        for r in range(0, rows, 8):
            for l in range(0, width, 128):
                small += squares[r:r + 8, l:l + 128]
        part[s] = small
        pl.when(last)(reduce_send)
        for p in range(planes):
            dt, dc = tb[s + 1, p], cb[s + 1, p]
            ways = [(fh[p], edge_rows(now, p), edge_rows(WARM + s, p), edge_rows(CURE + s, p),
                     edge_rows(FILL, p))]
            if p == 0:
                ways.append((fz[0], low_plane(now), low_plane(WARM + s), low_plane(CURE + s),
                             low_plane(FILL)))
            if p == planes - 1:
                ways.append((fz[planes], high_plane(now), high_plane(WARM + s),
                             high_plane(CURE + s), high_plane(FILL)))
            for way in ways:
                a, b = stream(p, *way)
                dt, dc = dt + a, dc + b
            share = fill[p] * clock_step_size
            t = tb[s, p] + share * dt
            c = cb[s, p] + share * dc
            tb[s + 1, p] = t
            cb[s + 1, p] = c
            mb[s + 1, p] = mobility_of(t, c, kb[p])
        pl.when(s < STEPS - 1)(lambda: send(MOB + s + 1, mb.at[s + 1]))
        return carry

    lax.fori_loop(0, STEPS, time_step, 0)

    outs = [
        pltpu.make_async_copy(pb.at[STEPS * SWEEPS], p_out, out_sem.at[0]),
        pltpu.make_async_copy(tb.at[STEPS], t_out, out_sem.at[1]),
        pltpu.make_async_copy(cb.at[STEPS], c_out, out_sem.at[2]),
    ]
    for copy in outs:
        copy.start()
    reduce_mid()

    def drain(m, carry):
        sent(m, pb.at[0])
        return carry

    lax.fori_loop(0, MESSAGES, drain, 0)
    reduce_end()
    for copy in outs:
        copy.wait()


def hand_over(t_in, c_in, p_in, rec_in, t_out, c_out, p_out, rec_out):
    t_out[...] = t_in[...]
    c_out[...] = c_in[...]
    p_out[...] = p_in[...]
    for s in range(STEPS):
        rec_out[s] = rec_in[s]


def per_device(n_ply, n_tile, *fields):
    shape = fields[0].shape
    planes, rows, width = shape
    real = jnp.float32

    def block(*lead):
        return pltpu.VMEM((*lead, *shape), real)

    dma = pltpu.SemaphoreType.DMA
    scratch = [
        block(STEPS + 1), block(STEPS + 1), block(STEPS * SWEEPS + 1), block(STEPS + 1), block(),
        pltpu.VMEM((3, *shape), jnp.int32), block(), block(), block(), block(4),
        pltpu.VMEM((planes + 1, rows, width), real), block(2), block(2), block(), block(), block(),
        block(), pltpu.VMEM((STEPS, 8, 128), real),
        pltpu.VMEM((MESSAGES, 2, rows, width), real), block(MESSAGES),
        pltpu.VMEM((n_tile, STEPS, 8, 128), real), pltpu.VMEM((STEPS, 8, 128), real),
        pltpu.VMEM((n_ply, STEPS, 8, 128), real),
        dma((7,)), dma((3,)), dma((MESSAGES, 4)), dma((MESSAGES, 4)),
        dma((n_tile,)), dma((n_tile,)), dma((n_ply,)), dma((n_ply,)),
    ]
    out = jax.ShapeDtypeStruct(shape, real)
    anywhere = pl.BlockSpec(memory_space=pl.ANY)
    results = pl.pallas_call(
        functools.partial(kernel, n_ply, n_tile),
        out_shape=(out, out, out, jax.ShapeDtypeStruct((STEPS,), real)),
        in_specs=[anywhere] * 7,
        out_specs=(anywhere, anywhere, anywhere, pl.BlockSpec(memory_space=pltpu.SMEM)),
        scratch_shapes=scratch,
        compiler_params=pltpu.CompilerParams(
            collective_id=0, has_side_effects=True, vmem_limit_bytes=60 * 1024 * 1024
        ),
    )(*fields)
    scalars = pl.BlockSpec(memory_space=pltpu.SMEM)
    return pl.pallas_call(
        hand_over,
        out_shape=(out, out, out, jax.ShapeDtypeStruct((STEPS,), real)),
        in_specs=[pl.BlockSpec(memory_space=pltpu.VMEM)] * 3 + [scalars],
        out_specs=(*[pl.BlockSpec(memory_space=pltpu.VMEM)] * 3, scalars),
        compiler_params=pltpu.CompilerParams(vmem_limit_bytes=60 * 1024 * 1024),
    )(*results)


def solution(mesh):
    spec = P("ply", "tile", None)
    return jax.shard_map(
        functools.partial(per_device, mesh.shape["ply"], mesh.shape["tile"]),
        mesh=mesh,
        in_specs=(spec,) * 7,
        out_specs=(spec, spec, spec, P()),
        check_vma=False,
    )
```
